256 devices in a mesh: particle: 32 (over z_hi, x, core), tile: 8 (over z_lo, y).
Axes of the slice: x: 4, y: 4, z: 8 (z_hi: 4, z_lo: 2; z = z_hi * 2 + z_lo), core: 2. Of those that a mesh axis runs over, the one named last changes fastest.
Arguments:
- ensemble: float32 [32, 4, 128, 2048], P('particle', None, 'tile'), may hold values from -6 to 6
- ancestor: int32 [32], replicated, may hold values from 0 to 31
- velocity: float32 [2, 4, 128, 2048], P(None, None, 'tile'), may hold values from -0.3 to 0.3
- observed: float32 [4, 128, 2048], P(None, 'tile'), may hold values from -6 to 6
- nudge_gain: float32 [4, 128, 2048], P(None, 'tile'), may hold values from 0.05 to 0.3
- forcing: float32 [32, 4, 128, 2048], P('particle', None, 'tile'), may hold values from -4 to 4
Outputs:
- forecast: float32 [32, 4, 128, 2048], P('particle', None, 'tile')
The draws below stay inside these ranges and needn't reach their ends.
All inputs are finite; a program needn't handle non-finite values.
Results may differ from the reference program's by a relative error of at most 0.00002.
Values sent between devices are 32-bit elements; how exact they have to be, the bound alone decides.
A program may use at most 64 MiB of HBM per device.

```python
import math
import jax
import jax.numpy as jnp
import numpy as np

LEV = 4
COLS = 2048
ITERS = 3
PARTICLES = 32
NY = 128


def with_ends(values, rng, least, high):
    dims = values.shape
    spot = [jax.random.randint(jax.random.fold_in(rng, axis), (), 0, dims[axis]) for axis in range(len(dims))]
    values = values.at[tuple(spot)].set(least)
    longest = dims.index(max(dims))
    spot[longest] = (spot[longest] + 1) % dims[longest]
    return values.at[tuple(spot)].set(high)


def steps_of(key, shape, shards, smallest, largest):
    def one(position, parts):
        draws = jax.random.uniform(jax.random.fold_in(jax.random.fold_in(key, 6), position), (parts,), jnp.float32, smallest / len(shards), largest / len(shards))
        return jnp.repeat(jnp.exp(draws), shape[position] // parts).reshape((-1,) + (1,) * (len(shape) - position - 1))

    factor_of = one(*shards[0])
    for cut in shards[1:]:
        factor_of = factor_of * one(*cut)
    return factor_of


def rank_table(amount, slope):
    portions = [(1 << 20) // math.isqrt(grade ** slope) + 1 for grade in range(1, amount + 1)]
    spread = 1 + sum(portions) // (1 << 30)
    return np.cumsum(np.array([max(1, weight // spread) for weight in portions]))


def ranked(stream_key, dims, amount, skew):
    listing = rank_table(amount, skew)
    pick = jax.random.randint(jax.random.fold_in(stream_key, 1), dims, 0, int(listing[amount - 1]))
    rank = jnp.searchsorted(jnp.asarray(listing, jnp.int32), pick, side="right")
    return jax.random.permutation(jax.random.fold_in(stream_key, 2), amount)[rank].astype(jnp.int32)


def scatter_about(rng, shape, deviation, bound, pieces=(), dtype=jnp.bfloat16):
    entries = deviation * jax.random.normal(rng, shape, jnp.float32)
    if pieces:
        entries = entries * steps_of(rng, shape, pieces, -0.22, 0.18)
    return jnp.clip(entries, -bound, bound).astype(dtype)


def setup_inputs(seed: int = 0) -> dict:
    key_of = jax.random.split(jax.random.key(seed), 7)
    return {
        "ensemble": scatter_about(key_of[0], (PARTICLES, LEV, NY, COLS), 1.0, 6.0, ((0, 32), (2, 8)), jnp.float32),
        "ancestor": with_ends(ranked(key_of[1], (PARTICLES,), PARTICLES, 2), jax.random.fold_in(key_of[1], 3), 0, PARTICLES - 1).astype(jnp.int32),
        "velocity": jnp.clip(jax.random.uniform(key_of[2], (2, LEV, NY, COLS), jnp.float32, -0.3, 0.3) * steps_of(key_of[2], (2, LEV, NY, COLS), ((2, 8),), -0.4, 0.0), -0.3, 0.3),
        "observed": scatter_about(key_of[3], (LEV, NY, COLS), 1.0, 6.0, ((1, 8),), jnp.float32),
        "nudge_gain": jnp.clip(0.05 + 0.25 * jax.random.uniform(key_of[4], (LEV, NY, COLS), jnp.float32) ** steps_of(key_of[4], (LEV, NY, COLS), ((1, 8),), -0.2, 0.2), 0.05, 0.3),
        "forcing": scatter_about(key_of[5], (PARTICLES, LEV, NY, COLS), 0.3, 4.0, ((0, 32), (2, 8)), jnp.float32),
    }


def advance(field, cross, along, observed, nudge_gain, forcing):
    rows = field.shape[2]
    padded = jnp.pad(field, ((0, 0), (0, 0), (2, 2), (0, 0)))
    dy = (8.0 * (padded[:, :, 3:rows + 3] - padded[:, :, 1:rows + 1]) - (padded[:, :, 4:rows + 4] - padded[:, :, 0:rows])) / 12.0
    east = jnp.roll(field, -1, 3)
    west = jnp.roll(field, 1, 3)
    dx = (8.0 * (east - west) - (jnp.roll(field, -2, 3) - jnp.roll(field, 2, 3))) / 12.0
    lap = padded[:, :, 3:rows + 3] + padded[:, :, 1:rows + 1] + east + west - 4.0 * field
    upper = jnp.concatenate([field[:, 1:], field[:, -1:]], axis=1)
    lower = jnp.concatenate([field[:, :1], field[:, :-1]], axis=1)
    vmix = upper + lower - 2.0 * field
    return field - cross * dx - along * dy + 0.1 * lap + 0.1 * vmix + nudge_gain * (observed - field) + forcing


def reference(ensemble, ancestor, velocity, observed, nudge_gain, forcing):
    field = jnp.take(ensemble, ancestor.astype(jnp.int32), axis=0)
    for step in range(ITERS):
        field = advance(field, velocity[0], velocity[1], observed, nudge_gain, forcing)
    return field
```

```python
import functools

import jax
import jax.numpy as jnp
from jax import lax
from jax.experimental import pallas as pl
from jax.experimental.pallas import tpu as pltpu
from jax.sharding import PartitionSpec as P

ITERS = 3
MESH = pl.DeviceIdType.MESH
EDGE = 128
TOP = 8
BLOCKS = 2
SPAN = 512


def kernel(
    anc, ens, vel, obs, gain, forc, out,
    inboxes, outbox, u0, u1, u2, vx, vy, keep, add, raw_o, raw_f, head_s, tail_s, head_r, tail_r,
    load_sem, own_sem, s1, r1, s2, r2, hs_sem, hr_sem,
):
    n = lax.axis_size("particle")
    tiles = lax.axis_size("tile")
    me = lax.axis_index("particle")
    t = lax.axis_index("tile")
    levels, rows, cols = obs.shape
    halves = rows // 8
    width = cols // BLOCKS
    cw = width * levels * halves // n
    per_row = width // cw
    fields = (u0, u1, u2)
    has_up, has_down = t > 0, t < tiles - 1

    loads = [
        pltpu.make_async_copy(vel.at[0], vx, load_sem.at[0]),
        pltpu.make_async_copy(vel.at[1], vy, load_sem.at[1]),
        pltpu.make_async_copy(gain, keep, load_sem.at[2]),
        pltpu.make_async_copy(obs, raw_o, load_sem.at[3]),
        pltpu.make_async_copy(forc.at[0], raw_f, load_sem.at[4]),
    ]
    for load in loads:
        load.start()

    def place(j, b, top, left):
        level = j // (halves * per_row)
        half = (j // per_row) % halves
        return (
            level,
            pl.ds(pl.multiple_of(top + half * 8, 8), 8),
            pl.ds(pl.multiple_of(left + b * width + (j % per_row) * cw, 128), cw),
        )

    def partner(r):
        return (me + (r % 4) * (n // 4) + r // 4) % n

    barrier = pltpu.get_barrier_semaphore()

    def greet(r, carry):
        pl.semaphore_signal(barrier, inc=1, device_id={"particle": partner(r)}, device_id_type=MESH)
        return carry

    lax.fori_loop(1, n, greet, 0)

    @pl.when(has_up)
    def _():
        pl.semaphore_signal(barrier, inc=1, device_id={"tile": t - 1}, device_id_type=MESH)

    @pl.when(has_down)
    def _():
        pl.semaphore_signal(barrier, inc=1, device_id={"tile": t + 1}, device_id_type=MESH)

    pl.semaphore_wait(barrier, n - 1 + jnp.where(has_up, 1, 0) + jnp.where(has_down, 1, 0))

    own1 = []
    for b in range(BLOCKS):

        def spread(r, carry, b=b):
            j = partner(r)
            pltpu.make_async_remote_copy(
                src_ref=ens.at[(0,) + place(j, b, 0, 0)],
                dst_ref=inboxes[b].at[me],
                send_sem=s1.at[b],
                recv_sem=r1.at[b],
                device_id={"particle": j},
                device_id_type=MESH,
            ).start()
            return carry

        lax.fori_loop(1, n, spread, 0)
        copy = pltpu.make_async_copy(ens.at[(0,) + place(me, b, 0, 0)], inboxes[b].at[me], own_sem.at[b])
        copy.start()
        own1.append(copy)

    for load in loads:
        load.wait()

    def prepare(i, carry):
        c = pl.ds(pl.multiple_of(i * SPAN, 128), SPAN)
        for l in range(levels):
            g = keep[l, :, c]
            add[l, :, c] = g * raw_o[l, :, c] + raw_f[l, :, c]
            keep[l, :, c] = 0.4 - g
            vx[l, :, c] = vx[l, :, c] * (1.0 / 12.0)
            vy[l, :, c] = vy[l, :, c] * (1.0 / 12.0)
        return carry

    lax.fori_loop(0, cols // SPAN, prepare, 0)

    own2 = []
    for b in range(BLOCKS):
        whole = inboxes[b].at[pl.ds(0, n - 1)]
        pltpu.make_async_copy(whole, whole, r1.at[b]).wait()
        own1[b].wait()

        def choose(p, carry, b=b):
            outbox[b, p] = inboxes[b][anc[p]]
            return carry

        lax.fori_loop(0, n, choose, 0)

        def deliver(r, carry, b=b):
            p = partner(r)
            pltpu.make_async_remote_copy(
                src_ref=outbox.at[b, p],
                dst_ref=u0.at[place(me, b, TOP, EDGE)],
                send_sem=s2.at[b],
                recv_sem=r2.at[b],
                device_id={"particle": p},
                device_id_type=MESH,
            ).start()
            return carry

        lax.fori_loop(1, n, deliver, 0)
        copy = pltpu.make_async_copy(outbox.at[b, me], u0.at[place(me, b, TOP, EDGE)], own_sem.at[BLOCKS + b])
        copy.start()
        own2.append(copy)

    for b in range(BLOCKS):
        whole = inboxes[b].at[pl.ds(0, n - 1)]
        pltpu.make_async_copy(whole, whole, r2.at[b]).wait()
        own2[b].wait()

    centre = pl.ds(EDGE, cols)
    for step in range(ITERS):
        u = fields[step]

        up = pltpu.make_async_remote_copy(
            src_ref=head_s.at[step], dst_ref=tail_r.at[step],
            send_sem=hs_sem.at[2 * step], recv_sem=hr_sem.at[2 * step],
            device_id={"tile": t - 1}, device_id_type=MESH,
        )
        down = pltpu.make_async_remote_copy(
            src_ref=tail_s.at[step], dst_ref=head_r.at[step],
            send_sem=hs_sem.at[2 * step + 1], recv_sem=hr_sem.at[2 * step + 1],
            device_id={"tile": t + 1}, device_id_type=MESH,
        )
        for l in range(levels):
            head_s[step, 2 * l : 2 * l + 2, :] = u[l, TOP : TOP + 2, centre]
        pl.when(has_up)(up.start)
        for l in range(levels):
            tail_s[step, 2 * l : 2 * l + 2, :] = u[l, TOP + rows - 2 : TOP + rows, centre]
        pl.when(has_down)(down.start)

        for l in range(levels):
            u[l, TOP : TOP + rows, 0:EDGE] = u[l, TOP : TOP + rows, cols : cols + EDGE]
            u[l, TOP : TOP + rows, EDGE + cols :] = u[l, TOP : TOP + rows, EDGE : 2 * EDGE]

        @pl.when(has_up)
        def _(u=u, step=step, down=down):
            down.wait_recv()
            for l in range(levels):
                u[l, TOP - 2 : TOP, centre] = head_r[step, 2 * l : 2 * l + 2, :]

        @pl.when(jnp.logical_not(has_up))
        def _(u=u):
            for l in range(levels):
                u[l, TOP - 2 : TOP, centre] = jnp.zeros((2, cols), jnp.float32)

        @pl.when(has_down)
        def _(u=u, step=step, up=up):
            up.wait_recv()
            for l in range(levels):
                u[l, TOP + rows : TOP + rows + 2, centre] = tail_r[step, 2 * l : 2 * l + 2, :]

        @pl.when(jnp.logical_not(has_down))
        def _(u=u):
            for l in range(levels):
                u[l, TOP + rows : TOP + rows + 2, centre] = jnp.zeros((2, cols), jnp.float32)

        def advance(i, carry, u=u, step=step):
            c = pl.multiple_of(i * SPAN, 128)
            mid = pl.ds(pl.multiple_of(c + EDGE, 128), SPAN)
            own = pl.ds(c, SPAN)
            wide = SPAN + 2 * EDGE
            for half in range(halves):
                top = TOP + 8 * half
                here = [u[l, top : top + 8, mid] for l in range(levels)]
                for l in range(levels):
                    around = u[l, top : top + 8, pl.ds(c, wide)]
                    east = pltpu.roll(around, wide - 1, 1)[:, EDGE : EDGE + SPAN]
                    west = pltpu.roll(around, 1, 1)[:, EDGE : EDGE + SPAN]
                    east2 = pltpu.roll(around, wide - 2, 1)[:, EDGE : EDGE + SPAN]
                    west2 = pltpu.roll(around, 2, 1)[:, EDGE : EDGE + SPAN]
                    south = u[l, top + 1 : top + 9, mid]
                    north = u[l, top - 1 : top + 7, mid]
                    south2 = u[l, top + 2 : top + 10, mid]
                    north2 = u[l, top - 2 : top + 6, mid]
                    r = pl.ds(8 * half, 8)
                    mixed = (east + west) + (south + north) + (here[min(l + 1, levels - 1)] + here[max(l - 1, 0)])
                    value = (
                        keep[l, r, own] * here[l]
                        + add[l, r, own]
                        + 0.1 * mixed
                        + vx[l, r, own] * ((east2 - west2) - 8.0 * (east - west))
                        + vy[l, r, own] * ((south2 - north2) - 8.0 * (south - north))
                    )
                    if step == ITERS - 1:
                        out[0, l, r, own] = value
                    else:
                        fields[step + 1][l, top : top + 8, mid] = value
            return carry

        lax.fori_loop(0, cols // SPAN, advance, 0)

        pl.when(has_up)(up.wait_send)
        pl.when(has_down)(down.wait_send)

    for b in range(BLOCKS):
        whole = inboxes[b].at[pl.ds(0, n - 1)]
        pltpu.make_async_copy(whole, whole, s1.at[b]).wait()
        pltpu.make_async_copy(whole, whole, s2.at[b]).wait()


def shards(ensemble, ancestor, velocity, observed, nudge_gain, forcing):
    _, levels, rows, cols = ensemble.shape
    n = lax.axis_size("particle")
    chunk = cols // BLOCKS * levels * (rows // 8) // n
    strip = (levels, rows, cols)
    padded = (levels, rows + 2 * TOP, cols + 2 * EDGE)
    vmem = functools.partial(pltpu.VMEM, dtype=jnp.float32)
    anywhere = pl.BlockSpec(memory_space=pl.ANY)
    return pl.pallas_call(
        kernel,
        out_shape=jax.ShapeDtypeStruct(ensemble.shape, jnp.float32),
        in_specs=[pl.BlockSpec(memory_space=pltpu.SMEM)] + [anywhere] * 5,
        out_specs=pl.BlockSpec(memory_space=pltpu.VMEM),
        scratch_shapes=[
            [vmem((n, 8, chunk))] * BLOCKS, vmem((BLOCKS, n, 8, chunk)),
            vmem(padded), vmem(padded), vmem(padded),
            vmem(strip), vmem(strip), vmem(strip), vmem(strip), vmem(strip), vmem(strip),
            vmem((ITERS, 2 * levels, cols)), vmem((ITERS, 2 * levels, cols)),
            vmem((ITERS, 2 * levels, cols)), vmem((ITERS, 2 * levels, cols)),
            pltpu.SemaphoreType.DMA((5,)),
            pltpu.SemaphoreType.DMA((2 * BLOCKS,)),
            pltpu.SemaphoreType.DMA((BLOCKS,)),
            pltpu.SemaphoreType.DMA((BLOCKS,)),
            pltpu.SemaphoreType.DMA((BLOCKS,)),
            pltpu.SemaphoreType.DMA((BLOCKS,)),
            pltpu.SemaphoreType.DMA((2 * ITERS,)),
            pltpu.SemaphoreType.DMA((2 * ITERS,)),
        ],
        compiler_params=pltpu.CompilerParams(
            collective_id=0, has_side_effects=True, vmem_limit_bytes=32 << 20
        ),
    )(ancestor, ensemble, velocity, observed, nudge_gain, forcing)


def solution(mesh):
    placed = (
        P("particle", None, "tile", None),
        P(),
        P(None, None, "tile", None),
        P(None, "tile", None),
        P(None, "tile", None),
        P("particle", None, "tile", None),
    )
    return jax.shard_map(
        shards,
        mesh=mesh,
        in_specs=placed,
        out_specs=P("particle", None, "tile", None),
        check_vma=False,
    )
```

```python
import functools

import jax
import jax.numpy as jnp
from jax import lax
from jax.experimental import pallas as pl
from jax.experimental.pallas import tpu as pltpu
from jax.sharding import PartitionSpec as P

ITERS = 3
MESH = pl.DeviceIdType.MESH
LANES = 128
GROUP = 4
TILE = 8


def kernel(
    anc, ens, vel, obs, gain, forc, out,
    raw, state, inboxes, outbox, fields, last, vx, vy, keep, add,
    load_sem, s1, r1, s2, r2, hs, hr,
):
    n = lax.axis_size("particle")
    tiles = lax.axis_size("tile")
    me = lax.axis_index("particle")
    t = lax.axis_index("tile")
    levels, rows, cols = obs.shape
    pairs = rows * levels // TILE
    blocks = pairs // 2
    per_pair = n // 2
    strips = cols // LANES
    has_up, has_down = t > 0, t < tiles - 1

    sources = [ens.at[0], vel.at[0], vel.at[1], gain, obs, forc.at[0]]
    loads = [pltpu.make_async_copy(s, raw.at[i], load_sem.at[i]) for i, s in enumerate(sources)]
    for load in loads:
        load.start()

    def partner(r):
        return (me + (r % 4) * (n // 4) + r // 4) % n

    barrier = pltpu.get_barrier_semaphore()

    def greet(r, carry):
        pl.semaphore_signal(barrier, inc=1, device_id={"particle": partner(r)}, device_id_type=MESH)
        return carry

    lax.fori_loop(1, n, greet, 0)

    @pl.when(has_up)
    def _():
        pl.semaphore_signal(barrier, inc=1, device_id={"tile": t - 1}, device_id_type=MESH)

    @pl.when(has_down)
    def _():
        pl.semaphore_signal(barrier, inc=1, device_id={"tile": t + 1}, device_id_type=MESH)

    loads[0].wait()
    for k in range(strips):
        for l in range(levels):
            state[k, pl.ds(l, rows, stride=levels), :] = raw[0, l, :, LANES * k : LANES * (k + 1)]

    def piece(j, b, top):
        pair = b + (j // per_pair) * (pairs - 1 - 2 * b)
        return (j % per_pair, pl.ds(pl.multiple_of(top + pair * TILE, TILE), TILE))

    def scatter(b):
        def send(r, carry):
            j = partner(r)
            pltpu.make_async_remote_copy(
                src_ref=state.at[piece(j, b, 0)],
                dst_ref=inboxes[b].at[me],
                send_sem=s1.at[b],
                recv_sem=r1.at[b],
                device_id={"particle": j},
                device_id_type=MESH,
            ).start()
            return carry

        lax.fori_loop(1, n, send, 0)
        inboxes[b][me] = state[piece(me, b, 0)]

    def all_of(b, sem):
        whole = inboxes[b].at[pl.ds(0, n - 1)]
        pltpu.make_async_copy(whole, whole, sem.at[b]).wait()

    def deliver(b):
        all_of(b, r1)
        for p in range(n):
            outbox[b, p] = inboxes[b][anc[p]]

        def send(r, carry):
            p = partner(r)
            pltpu.make_async_remote_copy(
                src_ref=outbox.at[b, p],
                dst_ref=fields[0].at[piece(me, b, TILE)],
                send_sem=s2.at[b],
                recv_sem=r2.at[b],
                device_id={"particle": p},
                device_id_type=MESH,
            ).start()
            return carry

        lax.fori_loop(1, n, send, 0)
        fields[0][piece(me, b, TILE)] = outbox[b, me]

    def halos(step):
        u = fields[step]
        up = pltpu.make_async_remote_copy(
            src_ref=u.at[:, pl.ds(TILE, TILE)],
            dst_ref=u.at[:, pl.ds(TILE * (pairs + 1), TILE)],
            send_sem=hs.at[2 * step], recv_sem=hr.at[2 * step],
            device_id={"tile": t - 1}, device_id_type=MESH,
        )
        down = pltpu.make_async_remote_copy(
            src_ref=u.at[:, pl.ds(TILE * pairs, TILE)],
            dst_ref=u.at[:, pl.ds(0, TILE)],
            send_sem=hs.at[2 * step + 1], recv_sem=hr.at[2 * step + 1],
            device_id={"tile": t + 1}, device_id_type=MESH,
        )
        return up, down

    def send_halos(step):
        up, down = halos(step)
        pl.when(has_up)(up.start)
        pl.when(has_down)(down.start)

    def wait_halos(step):
        up, down = halos(step)
        pl.when(has_up)(down.wait_recv)
        pl.when(has_down)(up.wait_recv)

    def advance(step, some):
        u = fields[step]

        def group(i, carry):
            level = lax.broadcasted_iota(jnp.int32, (TILE, LANES), 0) % levels
            lane = lax.broadcasted_iota(jnp.int32, (TILE, LANES), 1)
            first = i * GROUP
            ks = [(first + strips - 1) % strips] + [first + k for k in range(GROUP)] + [(first + GROUP) % strips]
            for pair in some:
                top = TILE * (pair + 1)
                r = pl.ds(TILE * pair, TILE)
                row = [u[k, top : top + TILE, :] for k in ks]
                left = [pltpu.roll(x, LANES - 1, 1) for x in row[1:]]
                left2 = [pltpu.roll(x, LANES - 2, 1) for x in row[1:]]
                right = [pltpu.roll(x, 1, 1) for x in row[:-1]]
                right2 = [pltpu.roll(x, 2, 1) for x in row[:-1]]
                for g in range(GROUP):
                    k = first + g
                    here = row[g + 1]
                    east = jnp.where(lane < LANES - 1, left[g], left[g + 1])
                    east2 = jnp.where(lane < LANES - 2, left2[g], left2[g + 1])
                    west = jnp.where(lane < 1, right[g], right[g + 1])
                    west2 = jnp.where(lane < 2, right2[g], right2[g + 1])
                    south = u[k, top + levels : top + TILE + levels, :]
                    north = u[k, top - levels : top + TILE - levels, :]
                    south2 = u[k, top + TILE : top + 2 * TILE, :]
                    north2 = u[k, top - TILE : top, :]
                    upper = jnp.where(level == levels - 1, here, pltpu.roll(here, TILE - 1, 0))
                    lower = jnp.where(level == 0, here, pltpu.roll(here, 1, 0))
                    mixed = (east + west) + (south + north) + (upper + lower)
                    value = (
                        keep[k, r, :] * here
                        + add[k, r, :]
                        + 0.1 * mixed
                        + vx[k, r, :] * ((east2 - west2) - 8.0 * (east - west))
                        + vy[k, r, :] * ((south2 - north2) - 8.0 * (south - north))
                    )
                    if step == ITERS - 1:
                        last[k, r, :] = value
                    else:
                        fields[step + 1][k, top : top + TILE, :] = value
            return carry

        lax.fori_loop(0, strips // GROUP, group, 0)

    pl.semaphore_wait(barrier, n - 1 + jnp.where(has_up, 1, 0) + jnp.where(has_down, 1, 0))

    scatter(0)
    scatter(1)

    for u in fields:

        @pl.when(jnp.logical_not(has_up))
        def _(u=u):
            u[:, 0:TILE, :] = jnp.zeros((strips, TILE, LANES), jnp.float32)

        @pl.when(jnp.logical_not(has_down))
        def _(u=u):
            u[:, TILE * (pairs + 1) :, :] = jnp.zeros((strips, TILE, LANES), jnp.float32)

    for load in loads[1:]:
        load.wait()

    for k in range(strips):
        c = slice(LANES * k, LANES * (k + 1))
        for l in range(levels):
            r = pl.ds(l, rows, stride=levels)
            vx[k, r, :] = raw[1, l, :, c] * (1.0 / 12.0)
            vy[k, r, :] = raw[2, l, :, c] * (1.0 / 12.0)
            keep[k, r, :] = 0.4 - raw[3, l, :, c]
            add[k, r, :] = raw[3, l, :, c] * raw[4, l, :, c] + raw[5, l, :, c]

    deliver(0)
    scatter(2)
    deliver(1)
    scatter(3)
    all_of(0, r2)
    send_halos(0)
    deliver(2)
    all_of(1, r2)
    wait_halos(0)
    advance(0, (0, pairs - 1))
    send_halos(1)
    deliver(3)
    all_of(2, r2)
    advance(0, (1, pairs - 2))
    wait_halos(1)
    advance(1, (0, pairs - 1))
    send_halos(2)
    all_of(3, r2)
    advance(0, range(2, pairs - 2))
    advance(1, range(1, pairs - 1))
    wait_halos(2)
    advance(2, range(pairs))
    for k in range(strips):
        for l in range(levels):
            out[0, l, :, LANES * k : LANES * (k + 1)] = last[k, pl.ds(l, rows, stride=levels), :]

    for step in range(ITERS):
        up, down = halos(step)
        pl.when(has_up)(up.wait_send)
        pl.when(has_down)(down.wait_send)
    for b in range(blocks):
        all_of(b, s1)
        all_of(b, s2)


def shards(ensemble, ancestor, velocity, observed, nudge_gain, forcing):
    _, levels, rows, cols = ensemble.shape
    n = lax.axis_size("particle")
    blocks = rows * levels // TILE // 2
    strip = (cols // LANES, rows * levels, LANES)
    padded = (cols // LANES, rows * levels + 2 * TILE, LANES)
    vmem = functools.partial(pltpu.VMEM, dtype=jnp.float32)
    anywhere = pl.BlockSpec(memory_space=pl.ANY)
    dma = pltpu.SemaphoreType.DMA
    return pl.pallas_call(
        kernel,
        out_shape=jax.ShapeDtypeStruct(ensemble.shape, jnp.float32),
        in_specs=[pl.BlockSpec(memory_space=pltpu.SMEM)] + [anywhere] * 5,
        out_specs=pl.BlockSpec(memory_space=pltpu.VMEM),
        scratch_shapes=[
            vmem((6, levels, rows, cols)),
            vmem(strip),
            [vmem((n, TILE, LANES))] * blocks,
            vmem((blocks, n, TILE, LANES)),
            [vmem(padded)] * ITERS,
            vmem(strip),
            vmem(strip), vmem(strip), vmem(strip), vmem(strip),
            dma((6,)), dma((blocks,)), dma((blocks,)), dma((blocks,)), dma((blocks,)),
            dma((2 * ITERS,)), dma((2 * ITERS,)),
        ],
        compiler_params=pltpu.CompilerParams(
            collective_id=0, has_side_effects=True, vmem_limit_bytes=60 << 20
        ),
    )(ancestor, ensemble, velocity, observed, nudge_gain, forcing)


def solution(mesh):
    placed = (
        P("particle", None, "tile", None),
        P(),
        P(None, None, "tile", None),
        P(None, "tile", None),
        P(None, "tile", None),
        P("particle", None, "tile", None),
    )
    return jax.shard_map(
        shards,
        mesh=mesh,
        in_specs=placed,
        out_specs=P("particle", None, "tile", None),
        check_vma=False,
    )
```

```python
import functools

import jax
import jax.numpy as jnp
from jax import lax
from jax.experimental import pallas as pl
from jax.experimental.pallas import tpu as pltpu
from jax.sharding import PartitionSpec as P

ITERS = 3
MESH = pl.DeviceIdType.MESH
LANES = 128
GROUP = 4
PARTS = 2
TILE = 8


def kernel(
    anc, ens, vel, obs, gain, forc, out,
    raw, state, inboxes, outbox, fields, last, vx, vy, keep, add,
    load_sem, s1, r1, s2, r2, hs, hr,
):
    n = lax.axis_size("particle")
    tiles = lax.axis_size("tile")
    me = lax.axis_index("particle")
    t = lax.axis_index("tile")
    levels, rows, cols = obs.shape
    pairs = rows * levels // TILE
    blocks = pairs // 2
    per_pair = n // 2
    strips = cols // LANES
    has_up, has_down = t > 0, t < tiles - 1

    sources = [ens.at[0], vel.at[0], vel.at[1], gain, obs, forc.at[0]]
    loads = [pltpu.make_async_copy(s, raw.at[i], load_sem.at[i]) for i, s in enumerate(sources)]
    for load in loads:
        load.start()

    def partner(r):
        return (me + (r % 4) * (n // 4) + r // 4) % n

    barrier = pltpu.get_barrier_semaphore()

    def greet(r, carry):
        pl.semaphore_signal(barrier, inc=1, device_id={"particle": partner(r)}, device_id_type=MESH)
        return carry

    lax.fori_loop(1, n, greet, 0)

    @pl.when(has_up)
    def _():
        pl.semaphore_signal(barrier, inc=1, device_id={"tile": t - 1}, device_id_type=MESH)

    @pl.when(has_down)
    def _():
        pl.semaphore_signal(barrier, inc=1, device_id={"tile": t + 1}, device_id_type=MESH)

    loads[0].wait()
    for k in range(strips):
        for l in range(levels):
            state[k, pl.ds(l, rows, stride=levels), :] = raw[0, l, :, LANES * k : LANES * (k + 1)]

    def piece(j, b, top):
        pair = b + (j // per_pair) * (pairs - 1 - 2 * b)
        return (j % per_pair, pl.ds(pl.multiple_of(top + pair * TILE, TILE), TILE))

    def scatter(b):
        def send(r, carry):
            j = partner(r)
            pltpu.make_async_remote_copy(
                src_ref=state.at[piece(j, b, 0)],
                dst_ref=inboxes[b].at[me],
                send_sem=s1.at[b],
                recv_sem=r1.at[b],
                device_id={"particle": j},
                device_id_type=MESH,
            ).start()
            return carry

        lax.fori_loop(1, n, send, 0)
        inboxes[b][me] = state[piece(me, b, 0)]

    def all_of(b, sem):
        whole = inboxes[b].at[pl.ds(0, n - 1)]
        pltpu.make_async_copy(whole, whole, sem.at[b]).wait()

    def deliver(b):
        all_of(b, r1)
        for p in range(n):
            outbox[b, p] = inboxes[b][anc[p]]

        def send(r, carry):
            p = partner(r)
            pltpu.make_async_remote_copy(
                src_ref=outbox.at[b, p],
                dst_ref=fields[0].at[piece(me, b, TILE)],
                send_sem=s2.at[b],
                recv_sem=r2.at[b],
                device_id={"particle": p},
                device_id_type=MESH,
            ).start()
            return carry

        lax.fori_loop(1, n, send, 0)
        fields[0][piece(me, b, TILE)] = outbox[b, me]

    def halos(step, part):
        u = fields[step]
        sem = 2 * (PARTS * step + part)
        c = pl.ds(part * (strips // PARTS), strips // PARTS)
        up = pltpu.make_async_remote_copy(
            src_ref=u.at[c, pl.ds(TILE, TILE)],
            dst_ref=u.at[c, pl.ds(TILE * (pairs + 1), TILE)],
            send_sem=hs.at[sem], recv_sem=hr.at[sem],
            device_id={"tile": t - 1}, device_id_type=MESH,
        )
        down = pltpu.make_async_remote_copy(
            src_ref=u.at[c, pl.ds(TILE * pairs, TILE)],
            dst_ref=u.at[c, pl.ds(0, TILE)],
            send_sem=hs.at[sem + 1], recv_sem=hr.at[sem + 1],
            device_id={"tile": t + 1}, device_id_type=MESH,
        )
        return up, down

    def send_halos(step, part):
        up, down = halos(step, part)
        pl.when(has_up)(up.start)
        pl.when(has_down)(down.start)

    def wait_halos(step, part):
        up, down = halos(step, part)
        pl.when(has_up)(down.wait_recv)
        pl.when(has_down)(up.wait_recv)

    def advance(step, some, part=0, parts=1):
        u = fields[step]

        def group(i, carry):
            level = lax.broadcasted_iota(jnp.int32, (TILE, LANES), 0) % levels
            lane = lax.broadcasted_iota(jnp.int32, (TILE, LANES), 1)
            first = i * GROUP
            ks = [(first + strips - 1) % strips] + [first + k for k in range(GROUP)] + [(first + GROUP) % strips]
            for pair in some:
                top = TILE * (pair + 1)
                r = pl.ds(TILE * pair, TILE)
                row = [u[k, top : top + TILE, :] for k in ks]
                left = [pltpu.roll(x, LANES - 1, 1) for x in row[1:]]
                left2 = [pltpu.roll(x, LANES - 2, 1) for x in row[1:]]
                right = [pltpu.roll(x, 1, 1) for x in row[:-1]]
                right2 = [pltpu.roll(x, 2, 1) for x in row[:-1]]
                for g in range(GROUP):
                    k = first + g
                    here = row[g + 1]
                    east = jnp.where(lane < LANES - 1, left[g], left[g + 1])
                    east2 = jnp.where(lane < LANES - 2, left2[g], left2[g + 1])
                    west = jnp.where(lane < 1, right[g], right[g + 1])
                    west2 = jnp.where(lane < 2, right2[g], right2[g + 1])
                    south = u[k, top + levels : top + TILE + levels, :]
                    north = u[k, top - levels : top + TILE - levels, :]
                    south2 = u[k, top + TILE : top + 2 * TILE, :]
                    north2 = u[k, top - TILE : top, :]
                    upper = jnp.where(level == levels - 1, here, pltpu.roll(here, TILE - 1, 0))
                    lower = jnp.where(level == 0, here, pltpu.roll(here, 1, 0))
                    mixed = (east + west) + (south + north) + (upper + lower)
                    value = (
                        keep[k, r, :] * here
                        + add[k, r, :]
                        + 0.1 * mixed
                        + vx[k, r, :] * ((east2 - west2) - 8.0 * (east - west))
                        + vy[k, r, :] * ((south2 - north2) - 8.0 * (south - north))
                    )
                    if step == ITERS - 1:
                        last[k, r, :] = value
                    else:
                        fields[step + 1][k, top : top + TILE, :] = value
            return carry

        groups = strips // GROUP // parts
        lax.fori_loop(part * groups, (part + 1) * groups, group, 0)

    pl.semaphore_wait(barrier, n - 1 + jnp.where(has_up, 1, 0) + jnp.where(has_down, 1, 0))

    scatter(0)
    scatter(1)
    scatter(2)

    for u in fields:

        @pl.when(jnp.logical_not(has_up))
        def _(u=u):
            u[:, 0:TILE, :] = jnp.zeros((strips, TILE, LANES), jnp.float32)

        @pl.when(jnp.logical_not(has_down))
        def _(u=u):
            u[:, TILE * (pairs + 1) :, :] = jnp.zeros((strips, TILE, LANES), jnp.float32)

    for load in loads[1:]:
        load.wait()

    for k in range(strips):
        c = slice(LANES * k, LANES * (k + 1))
        for l in range(levels):
            r = pl.ds(l, rows, stride=levels)
            vx[k, r, :] = raw[1, l, :, c] * (1.0 / 12.0)
            vy[k, r, :] = raw[2, l, :, c] * (1.0 / 12.0)
            keep[k, r, :] = 0.4 - raw[3, l, :, c]
            add[k, r, :] = raw[3, l, :, c] * raw[4, l, :, c] + raw[5, l, :, c]

    edges = (0, pairs - 1)
    deliver(0)
    scatter(3)
    deliver(1)
    deliver(2)
    all_of(0, r2)
    for part in range(PARTS):
        send_halos(0, part)
    deliver(3)
    all_of(1, r2)
    for part in range(PARTS):
        wait_halos(0, part)
        advance(0, edges, part, PARTS)
        send_halos(1, part)
    all_of(2, r2)
    advance(0, (1, pairs - 2))
    for part in range(PARTS):
        wait_halos(1, part)
        advance(1, edges, part, PARTS)
        send_halos(2, part)
    all_of(3, r2)
    advance(0, range(2, pairs - 2))
    advance(1, range(1, pairs - 1))
    advance(2, range(1, pairs - 1))
    for part in range(PARTS):
        wait_halos(2, part)
        advance(2, edges, part, PARTS)
    for k in range(strips):
        for l in range(levels):
            out[0, l, :, LANES * k : LANES * (k + 1)] = last[k, pl.ds(l, rows, stride=levels), :]

    for step in range(ITERS):
        for part in range(PARTS):
            up, down = halos(step, part)
            pl.when(has_up)(up.wait_send)
            pl.when(has_down)(down.wait_send)
    for b in range(blocks):
        all_of(b, s1)
        all_of(b, s2)


def shards(ensemble, ancestor, velocity, observed, nudge_gain, forcing):
    _, levels, rows, cols = ensemble.shape
    n = lax.axis_size("particle")
    blocks = rows * levels // TILE // 2
    strip = (cols // LANES, rows * levels, LANES)
    padded = (cols // LANES, rows * levels + 2 * TILE, LANES)
    vmem = functools.partial(pltpu.VMEM, dtype=jnp.float32)
    anywhere = pl.BlockSpec(memory_space=pl.ANY)
    dma = pltpu.SemaphoreType.DMA
    return pl.pallas_call(
        kernel,
        out_shape=pltpu.VMEM(ensemble.shape, jnp.float32),
        in_specs=[pl.BlockSpec(memory_space=pltpu.SMEM)] + [anywhere] * 5,
        out_specs=pl.BlockSpec(memory_space=pltpu.VMEM),
        scratch_shapes=[
            vmem((6, levels, rows, cols)),
            vmem(strip),
            [vmem((n, TILE, LANES))] * blocks,
            vmem((blocks, n, TILE, LANES)),
            [vmem(padded)] * ITERS,
            vmem(strip),
            vmem(strip), vmem(strip), vmem(strip), vmem(strip),
            dma((6,)), dma((blocks,)), dma((blocks,)), dma((blocks,)), dma((blocks,)),
            dma((2 * ITERS * PARTS,)), dma((2 * ITERS * PARTS,)),
        ],
        compiler_params=pltpu.CompilerParams(
            collective_id=0, has_side_effects=True, vmem_limit_bytes=60 << 20
        ),
    )(ancestor, ensemble, velocity, observed, nudge_gain, forcing)


def solution(mesh):
    placed = (
        P("particle", None, "tile", None),
        P(),
        P(None, None, "tile", None),
        P(None, "tile", None),
        P(None, "tile", None),
        P("particle", None, "tile", None),
    )
    return jax.shard_map(
        shards,
        mesh=mesh,
        in_specs=placed,
        out_specs=P("particle", None, "tile", None),
        check_vma=False,
    )
```

```python
import functools

import jax
import jax.numpy as jnp
from jax import lax
from jax.experimental import pallas as pl
from jax.experimental.pallas import tpu as pltpu
from jax.sharding import PartitionSpec as P

ITERS = 3
MESH = pl.DeviceIdType.MESH
LANES = 128
GROUP = 4
PARTS = 4
TILE = 8


def kernel(
    anc, ens, vel, obs, gain, forc, out,
    raw, state, inboxes, outbox, fields, last, vx, vy, keep, add,
    load_sem, s1, r1, s2, r2, hs, hr,
):
    n = lax.axis_size("particle")
    tiles = lax.axis_size("tile")
    me = lax.axis_index("particle")
    t = lax.axis_index("tile")
    levels, rows, cols = obs.shape
    pairs = rows * levels // TILE
    blocks = pairs // 2
    per_pair = n // 2
    strips = cols // LANES
    has_up, has_down = t > 0, t < tiles - 1

    sources = [ens.at[0], vel.at[0], vel.at[1], gain, obs, forc.at[0]]
    loads = [pltpu.make_async_copy(s, raw.at[i], load_sem.at[i]) for i, s in enumerate(sources)]
    for load in loads:
        load.start()

    def partner(r):
        return (me + (r % 4) * (n // 4) + r // 4) % n

    barrier = pltpu.get_barrier_semaphore()

    def greet(r, carry):
        pl.semaphore_signal(barrier, inc=1, device_id={"particle": partner(r)}, device_id_type=MESH)
        return carry

    lax.fori_loop(1, n, greet, 0)

    @pl.when(has_up)
    def _():
        pl.semaphore_signal(barrier, inc=1, device_id={"tile": t - 1}, device_id_type=MESH)

    @pl.when(has_down)
    def _():
        pl.semaphore_signal(barrier, inc=1, device_id={"tile": t + 1}, device_id_type=MESH)

    loads[0].wait()
    for k in range(strips):
        for l in range(levels):
            state[k, pl.ds(l, rows, stride=levels), :] = raw[0, l, :, LANES * k : LANES * (k + 1)]

    def piece(j, b, top):
        pair = b + (j % 2) * (pairs - 1 - 2 * b)
        return (j // 2, pl.ds(pl.multiple_of(top + pair * TILE, TILE), TILE))

    outer_is_up = t < tiles // 2

    def inner_first(r):
        side = jnp.where(outer_is_up, 1, 0)
        side = side + (r // per_pair) * (1 - 2 * side)
        return (me // 2 + (r % 4) * 4 + r % per_pair // 4) % per_pair * 2 + side

    def scatter(b):
        def send(r, carry):
            j = inner_first(r)
            copy = pltpu.make_async_remote_copy(
                src_ref=state.at[piece(j, b, 0)],
                dst_ref=inboxes[b].at[me],
                send_sem=s1.at[b],
                recv_sem=r1.at[b],
                device_id={"particle": j},
                device_id_type=MESH,
            )
            pl.when(j != me)(copy.start)
            return carry

        lax.fori_loop(0, n, send, 0)
        inboxes[b][me] = state[piece(me, b, 0)]

    def all_of(b, sem):
        whole = inboxes[b].at[pl.ds(0, n - 1)]
        pltpu.make_async_copy(whole, whole, sem.at[b]).wait()

    def arrived(b):
        whole = inboxes[b].at[pl.ds(0, n - 1)]
        pltpu.make_async_copy(whole, whole, r2.at[b + 1]).wait()

    def side_arrived(side):
        for own in (0, 1):
            some = inboxes[0].at[pl.ds(0, per_pair - own)]
            pl.when((me % 2 == side) == (own == 1))(pltpu.make_async_copy(some, some, r2.at[side]).wait)

    def deliver(b):
        all_of(b, r1)
        for p in range(n):
            outbox[b, p] = inboxes[b][anc[p]]

        def send(r, carry):
            p = partner(r)
            pltpu.make_async_remote_copy(
                src_ref=outbox.at[b, p],
                dst_ref=fields[0].at[piece(me, b, TILE)],
                send_sem=s2.at[b],
                recv_sem=r2.at[me % 2 if b == 0 else b + 1],
                device_id={"particle": p},
                device_id_type=MESH,
            ).start()
            return carry

        lax.fori_loop(1, n, send, 0)
        fields[0][piece(me, b, TILE)] = outbox[b, me]

    def halo(step, part, is_up):
        u = fields[step]
        c = pl.ds(part * (strips // PARTS), strips // PARTS)
        sem = 2 * (PARTS * step + part)
        mine = jnp.where(is_up, TILE, TILE * pairs)
        there = jnp.where(is_up, TILE * (pairs + 1), 0)
        return pltpu.make_async_remote_copy(
            src_ref=u.at[c, pl.ds(pl.multiple_of(mine, TILE), TILE)],
            dst_ref=u.at[c, pl.ds(pl.multiple_of(there, TILE), TILE)],
            send_sem=hs.at[sem + jnp.where(is_up, 0, 1)],
            recv_sem=hr.at[sem + jnp.where(is_up, 0, 1)],
            device_id={"tile": jnp.where(is_up, t - 1, t + 1)},
            device_id_type=MESH,
        )

    def arrival(step, part, is_up):
        c = pl.ds(part * (strips // PARTS), strips // PARTS)
        rows_here = pl.ds(pl.multiple_of(jnp.where(is_up, 0, TILE * (pairs + 1)), TILE), TILE)
        region = fields[step].at[c, rows_here]
        return pltpu.make_async_copy(region, region, hr.at[2 * (PARTS * step + part) + jnp.where(is_up, 1, 0)])

    sides = (outer_is_up, jnp.logical_not(outer_is_up))

    def has(is_up):
        return jnp.where(is_up, t > 0, t < tiles - 1)

    def send_halos(step, part, is_up):
        pl.when(has(is_up))(halo(step, part, is_up).start)

    def edge(step, part, is_up):
        pl.when(has(is_up))(arrival(step, part, is_up).wait)
        pl.when(is_up)(lambda: advance(step, (0,), part, PARTS))
        pl.when(jnp.logical_not(is_up))(lambda: advance(step, (pairs - 1,), part, PARTS))
        if step < ITERS - 1:
            send_halos(step + 1, part, is_up)

    def advance(step, some, part=0, parts=1):
        u = fields[step]

        def group(i, carry):
            level = lax.broadcasted_iota(jnp.int32, (TILE, LANES), 0) % levels
            lane = lax.broadcasted_iota(jnp.int32, (TILE, LANES), 1)
            first = i * GROUP
            ks = [(first + strips - 1) % strips] + [first + k for k in range(GROUP)] + [(first + GROUP) % strips]
            for pair in some:
                top = TILE * (pair + 1)
                r = pl.ds(TILE * pair, TILE)
                row = [u[k, top : top + TILE, :] for k in ks]
                left = [pltpu.roll(x, LANES - 1, 1) for x in row[1:]]
                left2 = [pltpu.roll(x, LANES - 2, 1) for x in row[1:]]
                right = [pltpu.roll(x, 1, 1) for x in row[:-1]]
                right2 = [pltpu.roll(x, 2, 1) for x in row[:-1]]
                for g in range(GROUP):
                    k = first + g
                    here = row[g + 1]
                    east = jnp.where(lane < LANES - 1, left[g], left[g + 1])
                    east2 = jnp.where(lane < LANES - 2, left2[g], left2[g + 1])
                    west = jnp.where(lane < 1, right[g], right[g + 1])
                    west2 = jnp.where(lane < 2, right2[g], right2[g + 1])
                    south = u[k, top + levels : top + TILE + levels, :]
                    north = u[k, top - levels : top + TILE - levels, :]
                    south2 = u[k, top + TILE : top + 2 * TILE, :]
                    north2 = u[k, top - TILE : top, :]
                    upper = jnp.where(level == levels - 1, here, pltpu.roll(here, TILE - 1, 0))
                    lower = jnp.where(level == 0, here, pltpu.roll(here, 1, 0))
                    mixed = (east + west) + (south + north) + (upper + lower)
                    value = (
                        keep[k, r, :] * here
                        + add[k, r, :]
                        + 0.1 * mixed
                        + vx[k, r, :] * ((east2 - west2) - 8.0 * (east - west))
                        + vy[k, r, :] * ((south2 - north2) - 8.0 * (south - north))
                    )
                    if step == ITERS - 1:
                        last[k, r, :] = value
                    else:
                        fields[step + 1][k, top : top + TILE, :] = value
            return carry

        groups = strips // GROUP // parts
        lax.fori_loop(part * groups, (part + 1) * groups, group, 0)

    pl.semaphore_wait(barrier, n - 1 + jnp.where(has_up, 1, 0) + jnp.where(has_down, 1, 0))

    scatter(0)
    scatter(1)
    scatter(2)
    for u in fields:

        @pl.when(jnp.logical_not(has_up))
        def _(u=u):
            u[:, 0:TILE, :] = jnp.zeros((strips, TILE, LANES), jnp.float32)

        @pl.when(jnp.logical_not(has_down))
        def _(u=u):
            u[:, TILE * (pairs + 1) :, :] = jnp.zeros((strips, TILE, LANES), jnp.float32)

    for load in loads[1:]:
        load.wait()

    for k in range(strips):
        c = slice(LANES * k, LANES * (k + 1))
        for l in range(levels):
            r = pl.ds(l, rows, stride=levels)
            vx[k, r, :] = raw[1, l, :, c] * (1.0 / 12.0)
            vy[k, r, :] = raw[2, l, :, c] * (1.0 / 12.0)
            keep[k, r, :] = 0.4 - raw[3, l, :, c]
            add[k, r, :] = raw[3, l, :, c] * raw[4, l, :, c] + raw[5, l, :, c]

    deliver(0)
    scatter(3)
    deliver(1)
    side_arrived(jnp.where(outer_is_up, 1, 0))
    for part in range(PARTS):
        send_halos(0, part, sides[1])
    deliver(2)
    side_arrived(jnp.where(outer_is_up, 0, 1))
    for part in range(PARTS):
        send_halos(0, part, sides[0])
    deliver(3)
    arrived(1)
    for side in sides:
        for part in range(PARTS):
            edge(0, part, side)
    arrived(2)
    advance(0, (1, pairs - 2))
    for side in sides:
        for part in range(PARTS):
            edge(1, part, side)
    arrived(3)
    advance(0, range(2, pairs - 2))
    advance(1, range(1, pairs - 1))
    advance(2, range(1, pairs - 1))
    for side in sides:
        for part in range(PARTS):
            edge(2, part, side)
    for k in range(strips):
        for l in range(levels):
            out[0, l, :, LANES * k : LANES * (k + 1)] = last[k, pl.ds(l, rows, stride=levels), :]

    for step in range(ITERS):
        for part in range(PARTS):
            for side in sides:
                pl.when(has(side))(halo(step, part, side).wait_send)
    for b in range(blocks):
        all_of(b, s1)
        all_of(b, s2)


def shards(ensemble, ancestor, velocity, observed, nudge_gain, forcing):
    _, levels, rows, cols = ensemble.shape
    n = lax.axis_size("particle")
    blocks = rows * levels // TILE // 2
    strip = (cols // LANES, rows * levels, LANES)
    padded = (cols // LANES, rows * levels + 2 * TILE, LANES)
    vmem = functools.partial(pltpu.VMEM, dtype=jnp.float32)
    anywhere = pl.BlockSpec(memory_space=pl.ANY)
    dma = pltpu.SemaphoreType.DMA
    return pl.pallas_call(
        kernel,
        out_shape=pltpu.VMEM(ensemble.shape, jnp.float32),
        in_specs=[pl.BlockSpec(memory_space=pltpu.SMEM)] + [anywhere] * 5,
        out_specs=pl.BlockSpec(memory_space=pltpu.VMEM),
        scratch_shapes=[
            vmem((6, levels, rows, cols)),
            vmem(strip),
            [vmem((n, TILE, LANES))] * blocks,
            vmem((blocks, n, TILE, LANES)),
            [vmem(padded)] * ITERS,
            vmem(strip),
            vmem(strip), vmem(strip), vmem(strip), vmem(strip),
            dma((6,)), dma((blocks,)), dma((blocks,)), dma((blocks,)), dma((blocks + 1,)),
            dma((2 * ITERS * PARTS,)), dma((2 * ITERS * PARTS,)),
        ],
        compiler_params=pltpu.CompilerParams(
            collective_id=0, has_side_effects=True, vmem_limit_bytes=60 << 20
        ),
    )(ancestor, ensemble, velocity, observed, nudge_gain, forcing)


def solution(mesh):
    placed = (
        P("particle", None, "tile", None),
        P(),
        P(None, None, "tile", None),
        P(None, "tile", None),
        P(None, "tile", None),
        P("particle", None, "tile", None),
    )
    return jax.shard_map(
        shards,
        mesh=mesh,
        in_specs=placed,
        out_specs=P("particle", None, "tile", None),
        check_vma=False,
    )
```

```python
import functools

import jax
import jax.numpy as jnp
from jax import lax
from jax.experimental import pallas as pl
from jax.experimental.pallas import tpu as pltpu
from jax.sharding import PartitionSpec as P

ITERS = 3
MESH = pl.DeviceIdType.MESH
LANES = 128
GROUP = 4
PARTS = 4
TILE = 8


def kernel(
    anc, ens, vel, obs, gain, forc, out,
    raw, state, inboxes, outbox, fields, last, vx, vy, keep, add,
    load_sem, s1, r1, s2, r2, hs, hr,
):
    n = lax.axis_size("particle")
    tiles = lax.axis_size("tile")
    me = lax.axis_index("particle")
    t = lax.axis_index("tile")
    levels, rows, cols = obs.shape
    pairs = rows * levels // TILE
    blocks = pairs // 2
    per_pair = n // 2
    strips = cols // LANES
    has_up, has_down = t > 0, t < tiles - 1

    sources = [ens.at[0], vel.at[0], vel.at[1], gain, obs, forc.at[0]]
    loads = [pltpu.make_async_copy(s, raw.at[i], load_sem.at[i]) for i, s in enumerate(sources)]
    for load in loads:
        load.start()

    def partner(r):
        return (me + (r % 4) * (n // 4) + r // 4) % n

    barrier = pltpu.get_barrier_semaphore()

    def greet(r, carry):
        pl.semaphore_signal(barrier, inc=1, device_id={"particle": partner(r)}, device_id_type=MESH)
        return carry

    lax.fori_loop(1, n, greet, 0)

    @pl.when(has_up)
    def _():
        pl.semaphore_signal(barrier, inc=1, device_id={"tile": t - 1}, device_id_type=MESH)

    @pl.when(has_down)
    def _():
        pl.semaphore_signal(barrier, inc=1, device_id={"tile": t + 1}, device_id_type=MESH)

    loads[0].wait()
    for k in range(strips):
        for l in range(levels):
            state[k, pl.ds(l, rows, stride=levels), :] = raw[0, l, :, LANES * k : LANES * (k + 1)]

    def piece(j, b, top):
        pair = b + (j % 2) * (pairs - 1 - 2 * b)
        return (j // 2, pl.ds(pl.multiple_of(top + pair * TILE, TILE), TILE))

    outer_is_up = t < tiles // 2

    def inner_first(r):
        side = jnp.where(outer_is_up, 1, 0)
        side = side + (r // per_pair) * (1 - 2 * side)
        return (me // 2 + (r % 4) * 4 + r % per_pair // 4) % per_pair * 2 + side

    def scatter(b):
        def send(r, carry):
            j = inner_first(r)
            copy = pltpu.make_async_remote_copy(
                src_ref=state.at[piece(j, b, 0)],
                dst_ref=inboxes[b].at[me],
                send_sem=s1.at[b],
                recv_sem=r1.at[b],
                device_id={"particle": j},
                device_id_type=MESH,
            )
            pl.when(j != me)(copy.start)
            return carry

        lax.fori_loop(0, n, send, 0)
        inboxes[b][me] = state[piece(me, b, 0)]

    def all_of(b, sem):
        whole = inboxes[b].at[pl.ds(0, n - 1)]
        pltpu.make_async_copy(whole, whole, sem.at[b]).wait()

    def arrived(b):
        whole = inboxes[b].at[pl.ds(0, n - 1)]
        pltpu.make_async_copy(whole, whole, r2.at[b + 1]).wait()

    def side_arrived(side):
        for own in (0, 1):
            some = inboxes[0].at[pl.ds(0, per_pair - own)]
            pl.when((me % 2 == side) == (own == 1))(pltpu.make_async_copy(some, some, r2.at[side]).wait)

    def deliver(b):
        all_of(b, r1)
        for p in range(n):
            outbox[b, p] = inboxes[b][anc[p]]

        def send(r, carry):
            p = partner(r)
            pltpu.make_async_remote_copy(
                src_ref=outbox.at[b, p],
                dst_ref=fields[0].at[piece(me, b, TILE)],
                send_sem=s2.at[b],
                recv_sem=r2.at[me % 2 if b == 0 else b + 1],
                device_id={"particle": p},
                device_id_type=MESH,
            ).start()
            return carry

        lax.fori_loop(1, n, send, 0)
        fields[0][piece(me, b, TILE)] = outbox[b, me]

    def halo(step, part, is_up):
        u = fields[step]
        c = pl.ds(part * (strips // PARTS), strips // PARTS)
        sem = 2 * (PARTS * step + part)
        mine = jnp.where(is_up, TILE, TILE * pairs)
        there = jnp.where(is_up, TILE * (pairs + 1), 0)
        return pltpu.make_async_remote_copy(
            src_ref=u.at[c, pl.ds(pl.multiple_of(mine, TILE), TILE)],
            dst_ref=u.at[c, pl.ds(pl.multiple_of(there, TILE), TILE)],
            send_sem=hs.at[sem + jnp.where(is_up, 0, 1)],
            recv_sem=hr.at[sem + jnp.where(is_up, 0, 1)],
            device_id={"tile": jnp.where(is_up, t - 1, t + 1)},
            device_id_type=MESH,
        )

    def arrival(step, part, is_up):
        c = pl.ds(part * (strips // PARTS), strips // PARTS)
        rows_here = pl.ds(pl.multiple_of(jnp.where(is_up, 0, TILE * (pairs + 1)), TILE), TILE)
        region = fields[step].at[c, rows_here]
        return pltpu.make_async_copy(region, region, hr.at[2 * (PARTS * step + part) + jnp.where(is_up, 1, 0)])

    sides = (outer_is_up, jnp.logical_not(outer_is_up))

    def has(is_up):
        return jnp.where(is_up, t > 0, t < tiles - 1)

    def send_halos(step, part, is_up):
        pl.when(has(is_up))(halo(step, part, is_up).start)

    def edge(step, part, is_up):
        pl.when(has(is_up))(arrival(step, part, is_up).wait)
        pl.when(is_up)(lambda: advance(step, (0,), part, PARTS))
        pl.when(jnp.logical_not(is_up))(lambda: advance(step, (pairs - 1,), part, PARTS))
        if step < ITERS - 1:
            send_halos(step + 1, part, is_up)

    def advance(step, some, part=0, parts=1):
        u = fields[step]
        size = GROUP if parts > 1 else 4 * GROUP

        def group(i, carry):
            level = lax.broadcasted_iota(jnp.int32, (TILE, LANES), 0) % levels
            lane = lax.broadcasted_iota(jnp.int32, (TILE, LANES), 1)
            first = i * size
            ks = [(first + strips - 1) % strips] + [first + k for k in range(size)] + [(first + size) % strips]
            for pair in some:
                top = TILE * (pair + 1)
                r = pl.ds(TILE * pair, TILE)
                row = [u[k, top : top + TILE, :] for k in ks]
                left = [pltpu.roll(x, LANES - 1, 1) for x in row[1:]]
                left2 = [pltpu.roll(x, LANES - 2, 1) for x in row[1:]]
                right = [pltpu.roll(x, 1, 1) for x in row[:-1]]
                right2 = [pltpu.roll(x, 2, 1) for x in row[:-1]]
                for g in range(size):
                    k = first + g
                    here = row[g + 1]
                    east = jnp.where(lane < LANES - 1, left[g], left[g + 1])
                    east2 = jnp.where(lane < LANES - 2, left2[g], left2[g + 1])
                    west = jnp.where(lane < 1, right[g], right[g + 1])
                    west2 = jnp.where(lane < 2, right2[g], right2[g + 1])
                    south = u[k, top + levels : top + TILE + levels, :]
                    north = u[k, top - levels : top + TILE - levels, :]
                    south2 = u[k, top + TILE : top + 2 * TILE, :]
                    north2 = u[k, top - TILE : top, :]
                    upper = jnp.where(level == levels - 1, here, pltpu.roll(here, TILE - 1, 0))
                    lower = jnp.where(level == 0, here, pltpu.roll(here, 1, 0))
                    mixed = (east + west) + (south + north) + (upper + lower)
                    value = (
                        keep[k, r, :] * here
                        + add[k, r, :]
                        + 0.1 * mixed
                        + vx[k, r, :] * ((east2 - west2) - 8.0 * (east - west))
                        + vy[k, r, :] * ((south2 - north2) - 8.0 * (south - north))
                    )
                    if step == ITERS - 1:
                        last[k, r, :] = value
                    else:
                        fields[step + 1][k, top : top + TILE, :] = value
            return carry

        groups = strips // size // parts
        lax.fori_loop(part * groups, (part + 1) * groups, group, 0)

    pl.semaphore_wait(barrier, n - 1 + jnp.where(has_up, 1, 0) + jnp.where(has_down, 1, 0))

    scatter(0)
    scatter(1)
    scatter(2)
    for u in fields:

        @pl.when(jnp.logical_not(has_up))
        def _(u=u):
            u[:, 0:TILE, :] = jnp.zeros((strips, TILE, LANES), jnp.float32)

        @pl.when(jnp.logical_not(has_down))
        def _(u=u):
            u[:, TILE * (pairs + 1) :, :] = jnp.zeros((strips, TILE, LANES), jnp.float32)

    for load in loads[1:]:
        load.wait()

    for k in range(strips):
        c = slice(LANES * k, LANES * (k + 1))
        for l in range(levels):
            r = pl.ds(l, rows, stride=levels)
            vx[k, r, :] = raw[1, l, :, c] * (1.0 / 12.0)
            vy[k, r, :] = raw[2, l, :, c] * (1.0 / 12.0)
            keep[k, r, :] = 0.4 - raw[3, l, :, c]
            add[k, r, :] = raw[3, l, :, c] * raw[4, l, :, c] + raw[5, l, :, c]

    deliver(0)
    scatter(3)
    deliver(1)
    side_arrived(jnp.where(outer_is_up, 1, 0))
    for part in range(PARTS):
        send_halos(0, part, sides[1])
    deliver(2)
    side_arrived(jnp.where(outer_is_up, 0, 1))
    for part in range(PARTS):
        send_halos(0, part, sides[0])
    deliver(3)
    arrived(1)
    for side in sides:
        for part in range(PARTS):
            edge(0, part, side)
    arrived(2)
    advance(0, (1, pairs - 2))
    for side in sides:
        for part in range(PARTS):
            edge(1, part, side)
    arrived(3)
    advance(0, range(2, pairs - 2))
    advance(1, range(1, pairs - 1))
    advance(2, range(1, pairs - 1))
    for side in sides:
        for part in range(PARTS):
            edge(2, part, side)
    for k in range(strips):
        for l in range(levels):
            out[0, l, :, LANES * k : LANES * (k + 1)] = last[k, pl.ds(l, rows, stride=levels), :]

    for step in range(ITERS):
        for part in range(PARTS):
            for side in sides:
                pl.when(has(side))(halo(step, part, side).wait_send)
    for b in range(blocks):
        all_of(b, s1)
        all_of(b, s2)


def shards(ensemble, ancestor, velocity, observed, nudge_gain, forcing):
    _, levels, rows, cols = ensemble.shape
    n = lax.axis_size("particle")
    blocks = rows * levels // TILE // 2
    strip = (cols // LANES, rows * levels, LANES)
    padded = (cols // LANES, rows * levels + 2 * TILE, LANES)
    vmem = functools.partial(pltpu.VMEM, dtype=jnp.float32)
    anywhere = pl.BlockSpec(memory_space=pl.ANY)
    dma = pltpu.SemaphoreType.DMA
    return pl.pallas_call(
        kernel,
        out_shape=pltpu.VMEM(ensemble.shape, jnp.float32),
        in_specs=[pl.BlockSpec(memory_space=pltpu.SMEM)] + [anywhere] * 5,
        out_specs=pl.BlockSpec(memory_space=pltpu.VMEM),
        scratch_shapes=[
            vmem((6, levels, rows, cols)),
            vmem(strip),
            [vmem((n, TILE, LANES))] * blocks,
            vmem((blocks, n, TILE, LANES)),
            [vmem(padded)] * ITERS,
            vmem(strip),
            vmem(strip), vmem(strip), vmem(strip), vmem(strip),
            dma((6,)), dma((blocks,)), dma((blocks,)), dma((blocks,)), dma((blocks + 1,)),
            dma((2 * ITERS * PARTS,)), dma((2 * ITERS * PARTS,)),
        ],
        compiler_params=pltpu.CompilerParams(
            collective_id=0, has_side_effects=True, vmem_limit_bytes=60 << 20
        ),
    )(ancestor, ensemble, velocity, observed, nudge_gain, forcing)


def solution(mesh):
    placed = (
        P("particle", None, "tile", None),
        P(),
        P(None, None, "tile", None),
        P(None, "tile", None),
        P(None, "tile", None),
        P("particle", None, "tile", None),
    )
    return jax.shard_map(
        shards,
        mesh=mesh,
        in_specs=placed,
        out_specs=P("particle", None, "tile", None),
        check_vma=False,
    )
```

```python
import functools

import jax
import jax.numpy as jnp
from jax import lax
from jax.experimental import pallas as pl
from jax.experimental.pallas import tpu as pltpu
from jax.sharding import PartitionSpec as P

ITERS = 3
MESH = pl.DeviceIdType.MESH
LANES = 128
GROUP = 4
PARTS = 4
TILE = 8


def kernel(
    anc, ens, vel, obs, gain, forc, out,
    raw, state, inboxes, outbox, fields, last, vx, vy, keep, add,
    load_sem, s1, r1, s2, r2, hs, hr,
):
    n = lax.axis_size("particle")
    tiles = lax.axis_size("tile")
    me = lax.axis_index("particle")
    t = lax.axis_index("tile")
    levels, rows, cols = obs.shape
    pairs = rows * levels // TILE
    blocks = pairs // 2
    per_pair = n // 2
    strips = cols // LANES
    has_up, has_down = t > 0, t < tiles - 1

    sources = [ens.at[0], vel.at[0], vel.at[1], gain, obs, forc.at[0]]
    loads = [pltpu.make_async_copy(s, raw.at[i], load_sem.at[i]) for i, s in enumerate(sources)]
    for load in loads:
        load.start()

    def partner(r):
        return (me + (r % 4) * (n // 4) + r // 4) % n

    barrier = pltpu.get_barrier_semaphore()

    def greet(r, carry):
        pl.semaphore_signal(barrier, inc=1, device_id={"particle": partner(r)}, device_id_type=MESH)
        return carry

    lax.fori_loop(1, n, greet, 0)

    @pl.when(has_up)
    def _():
        pl.semaphore_signal(barrier, inc=1, device_id={"tile": t - 1}, device_id_type=MESH)

    @pl.when(has_down)
    def _():
        pl.semaphore_signal(barrier, inc=1, device_id={"tile": t + 1}, device_id_type=MESH)

    loads[0].wait()
    for k in range(strips):
        for l in range(levels):
            state[k, pl.ds(l, rows, stride=levels), :] = raw[0, l, :, LANES * k : LANES * (k + 1)]

    def piece(j, b, top):
        pair = b + (j % 2) * (pairs - 1 - 2 * b)
        return (j // 2, pl.ds(pl.multiple_of(top + pair * TILE, TILE), TILE))

    outer_is_up = t < tiles // 2

    def inner_first(r):
        side = jnp.where(outer_is_up, 1, 0)
        side = side + (r // per_pair) * (1 - 2 * side)
        return (me // 2 + (r % 4) * 4 + r % per_pair // 4) % per_pair * 2 + side

    def scatter(b):
        def send(r, carry):
            j = inner_first(r)
            copy = pltpu.make_async_remote_copy(
                src_ref=state.at[piece(j, b, 0)],
                dst_ref=inboxes[b].at[me],
                send_sem=s1.at[b],
                recv_sem=r1.at[b],
                device_id={"particle": j},
                device_id_type=MESH,
            )
            pl.when(j != me)(copy.start)
            return carry

        lax.fori_loop(0, n, send, 0)
        inboxes[b][me] = state[piece(me, b, 0)]

    def all_of(b, sem):
        whole = inboxes[b].at[pl.ds(0, n - 1)]
        pltpu.make_async_copy(whole, whole, sem.at[b]).wait()

    def arrived(b):
        whole = inboxes[b].at[pl.ds(0, n - 1)]
        pltpu.make_async_copy(whole, whole, r2.at[b + 1]).wait()

    def side_arrived(side):
        for own in (0, 1):
            some = inboxes[0].at[pl.ds(0, per_pair - own)]
            pl.when((me % 2 == side) == (own == 1))(pltpu.make_async_copy(some, some, r2.at[side]).wait)

    def deliver(b):
        all_of(b, r1)
        for p in range(n):
            outbox[b, p] = inboxes[b][anc[p]]

        def send(r, carry):
            p = partner(r)
            pltpu.make_async_remote_copy(
                src_ref=outbox.at[b, p],
                dst_ref=fields[0].at[piece(me, b, TILE)],
                send_sem=s2.at[b],
                recv_sem=r2.at[me % 2 if b == 0 else b + 1],
                device_id={"particle": p},
                device_id_type=MESH,
            ).start()
            return carry

        lax.fori_loop(1, n, send, 0)
        fields[0][piece(me, b, TILE)] = outbox[b, me]

    def halo(step, part, is_up):
        u = fields[step]
        c = pl.ds(part * (strips // PARTS), strips // PARTS)
        sem = 2 * (PARTS * step + part)
        mine = jnp.where(is_up, TILE, TILE * pairs)
        there = jnp.where(is_up, TILE * (pairs + 1), 0)
        return pltpu.make_async_remote_copy(
            src_ref=u.at[c, pl.ds(pl.multiple_of(mine, TILE), TILE)],
            dst_ref=u.at[c, pl.ds(pl.multiple_of(there, TILE), TILE)],
            send_sem=hs.at[sem + jnp.where(is_up, 0, 1)],
            recv_sem=hr.at[sem + jnp.where(is_up, 0, 1)],
            device_id={"tile": jnp.where(is_up, t - 1, t + 1)},
            device_id_type=MESH,
        )

    def arrival(step, part, is_up):
        c = pl.ds(part * (strips // PARTS), strips // PARTS)
        rows_here = pl.ds(pl.multiple_of(jnp.where(is_up, 0, TILE * (pairs + 1)), TILE), TILE)
        region = fields[step].at[c, rows_here]
        return pltpu.make_async_copy(region, region, hr.at[2 * (PARTS * step + part) + jnp.where(is_up, 1, 0)])

    sides = (outer_is_up, jnp.logical_not(outer_is_up))

    def has(is_up):
        return jnp.where(is_up, t > 0, t < tiles - 1)

    def send_halos(step, part, is_up):
        pl.when(has(is_up))(halo(step, part, is_up).start)

    def finish(part, half):
        some = rows // 2
        for k in range(part * (strips // PARTS), (part + 1) * (strips // PARTS)):
            for l in range(levels):
                out[0, l, some * half : some * (half + 1), LANES * k : LANES * (k + 1)] = last[
                    k, pl.ds(some * levels * half + l, some, stride=levels), :
                ]

    def edge(step, part, is_up):
        pl.when(has(is_up))(arrival(step, part, is_up).wait)
        def side_step(pair, half):
            advance(step, (pair,), part, PARTS)
            if step == ITERS - 1:
                finish(part, half)

        pl.when(is_up)(lambda: side_step(0, 0))
        pl.when(jnp.logical_not(is_up))(lambda: side_step(pairs - 1, 1))
        if step < ITERS - 1:
            send_halos(step + 1, part, is_up)

    def advance(step, some, part=0, parts=1):
        u = fields[step]
        size = GROUP if parts > 1 else 4 * GROUP

        def group(i, carry):
            level = lax.broadcasted_iota(jnp.int32, (TILE, LANES), 0) % levels
            lane = lax.broadcasted_iota(jnp.int32, (TILE, LANES), 1)
            first = i * size
            ks = [(first + strips - 1) % strips] + [first + k for k in range(size)] + [(first + size) % strips]
            for pair in some:
                top = TILE * (pair + 1)
                r = pl.ds(TILE * pair, TILE)
                row = [u[k, top : top + TILE, :] for k in ks]
                left = [pltpu.roll(x, LANES - 1, 1) for x in row[1:]]
                left2 = [pltpu.roll(x, LANES - 2, 1) for x in row[1:]]
                right = [pltpu.roll(x, 1, 1) for x in row[:-1]]
                right2 = [pltpu.roll(x, 2, 1) for x in row[:-1]]
                for g in range(size):
                    k = first + g
                    here = row[g + 1]
                    east = jnp.where(lane < LANES - 1, left[g], left[g + 1])
                    east2 = jnp.where(lane < LANES - 2, left2[g], left2[g + 1])
                    west = jnp.where(lane < 1, right[g], right[g + 1])
                    west2 = jnp.where(lane < 2, right2[g], right2[g + 1])
                    south = u[k, top + levels : top + TILE + levels, :]
                    north = u[k, top - levels : top + TILE - levels, :]
                    south2 = u[k, top + TILE : top + 2 * TILE, :]
                    north2 = u[k, top - TILE : top, :]
                    upper = jnp.where(level == levels - 1, here, pltpu.roll(here, TILE - 1, 0))
                    lower = jnp.where(level == 0, here, pltpu.roll(here, 1, 0))
                    mixed = (east + west) + (south + north) + (upper + lower)
                    value = (
                        keep[k, r, :] * here
                        + add[k, r, :]
                        + 0.1 * mixed
                        + vx[k, r, :] * ((east2 - west2) - 8.0 * (east - west))
                        + vy[k, r, :] * ((south2 - north2) - 8.0 * (south - north))
                    )
                    if step == ITERS - 1:
                        last[k, r, :] = value
                    else:
                        fields[step + 1][k, top : top + TILE, :] = value
            return carry

        groups = strips // size // parts
        lax.fori_loop(part * groups, (part + 1) * groups, group, 0)

    pl.semaphore_wait(barrier, n - 1 + jnp.where(has_up, 1, 0) + jnp.where(has_down, 1, 0))

    scatter(0)
    scatter(1)
    scatter(2)
    for u in fields:

        @pl.when(jnp.logical_not(has_up))
        def _(u=u):
            u[:, 0:TILE, :] = jnp.zeros((strips, TILE, LANES), jnp.float32)

        @pl.when(jnp.logical_not(has_down))
        def _(u=u):
            u[:, TILE * (pairs + 1) :, :] = jnp.zeros((strips, TILE, LANES), jnp.float32)

    for load in loads[1:]:
        load.wait()

    for k in range(strips):
        c = slice(LANES * k, LANES * (k + 1))
        for l in range(levels):
            r = pl.ds(l, rows, stride=levels)
            vx[k, r, :] = raw[1, l, :, c] * (1.0 / 12.0)
            vy[k, r, :] = raw[2, l, :, c] * (1.0 / 12.0)
            keep[k, r, :] = 0.4 - raw[3, l, :, c]
            add[k, r, :] = raw[3, l, :, c] * raw[4, l, :, c] + raw[5, l, :, c]

    deliver(0)
    scatter(3)
    deliver(1)
    side_arrived(jnp.where(outer_is_up, 1, 0))
    for part in range(PARTS):
        send_halos(0, part, sides[1])
    deliver(2)
    side_arrived(jnp.where(outer_is_up, 0, 1))
    for part in range(PARTS):
        send_halos(0, part, sides[0])
    deliver(3)
    arrived(1)
    for side in sides:
        for part in range(PARTS):
            edge(0, part, side)
    arrived(2)
    advance(0, (1, pairs - 2))
    for side in sides:
        for part in range(PARTS):
            edge(1, part, side)
    arrived(3)
    advance(0, range(2, pairs - 2))
    advance(1, range(1, pairs - 1))
    advance(2, range(1, pairs - 1))
    for side in sides:
        for part in range(PARTS):
            edge(2, part, side)

    for step in range(ITERS):
        for part in range(PARTS):
            for side in sides:
                pl.when(has(side))(halo(step, part, side).wait_send)
    for b in range(blocks):
        all_of(b, s1)
        all_of(b, s2)


def shards(ensemble, ancestor, velocity, observed, nudge_gain, forcing):
    _, levels, rows, cols = ensemble.shape
    n = lax.axis_size("particle")
    blocks = rows * levels // TILE // 2
    strip = (cols // LANES, rows * levels, LANES)
    padded = (cols // LANES, rows * levels + 2 * TILE, LANES)
    vmem = functools.partial(pltpu.VMEM, dtype=jnp.float32)
    anywhere = pl.BlockSpec(memory_space=pl.ANY)
    dma = pltpu.SemaphoreType.DMA
    return pl.pallas_call(
        kernel,
        out_shape=pltpu.VMEM(ensemble.shape, jnp.float32),
        in_specs=[pl.BlockSpec(memory_space=pltpu.SMEM)] + [anywhere] * 5,
        out_specs=pl.BlockSpec(memory_space=pltpu.VMEM),
        scratch_shapes=[
            vmem((6, levels, rows, cols)),
            vmem(strip),
            [vmem((n, TILE, LANES))] * blocks,
            vmem((blocks, n, TILE, LANES)),
            [vmem(padded)] * ITERS,
            vmem(strip),
            vmem(strip), vmem(strip), vmem(strip), vmem(strip),
            dma((6,)), dma((blocks,)), dma((blocks,)), dma((blocks,)), dma((blocks + 1,)),
            dma((2 * ITERS * PARTS,)), dma((2 * ITERS * PARTS,)),
        ],
        compiler_params=pltpu.CompilerParams(
            collective_id=0, has_side_effects=True, vmem_limit_bytes=60 << 20
        ),
    )(ancestor, ensemble, velocity, observed, nudge_gain, forcing)


def solution(mesh):
    placed = (
        P("particle", None, "tile", None),
        P(),
        P(None, None, "tile", None),
        P(None, "tile", None),
        P(None, "tile", None),
        P("particle", None, "tile", None),
    )
    return jax.shard_map(
        shards,
        mesh=mesh,
        in_specs=placed,
        out_specs=P("particle", None, "tile", None),
        check_vma=False,
    )
```
